768 devices in a mesh: grp: 16 (over y, core), dom: 48 (over z, x).
Axes of the slice: x: 4, y: 8, z: 12, core: 2. Of those that a mesh axis runs over, the one named last changes fastest.
Arguments:
- a_tiles: bfloat16 [3072, 8, 128, 128], P(('grp', 'dom')), may hold values from -0.1875 to 0.1875
- a_cols: int32 [3072, 8], P(('grp', 'dom')), may hold values from 0 to 12, as said below
- p_tiles: bfloat16 [3072, 128, 128], P(('grp', 'dom')), may hold values from -0.47851562 to 0.47851562
- send_list: int32 [768, 8], P(('grp', 'dom')), may hold values from 0 to 3
- term_slot: int32 [3072, 4, 8, 4], P(('grp', 'dom')), may hold values from 0 to 63
- owner_slot: int32 [49152], P(('grp', 'dom')), may hold values from 0 to 12287, as said below
Outputs:
- coarse: float32 [12288, 1024], P('dom')
The draws below stay inside these ranges and needn't reach their ends.
Inputs may be any that keep to these rules, and one draw needn't show every extreme that they name: `a_cols`: entries below 4 name local blocks; 4 + i names the i-th block received from the lower neighbour, 8 + i the i-th from the higher one, 12 the zero block. Every block row's first tile is local. The first device never names the lower neighbour's blocks and the last never the higher one's; every other device names some block of its lower neighbour and some block of its higher neighbour. `owner_slot`: an entry c names the coarse block owned by the device with dom index c // 256 and grp index (c // 16) % 16, the same grp index as the device that holds the entry. Of one device's 64 entries, at most 2 name blocks of any one owner, and exactly 2 do for some owner.
All inputs are finite; a program needn't handle non-finite values.
Results may differ from the reference program's by a relative error of at most 0.0029.
Values may be sent and summed in bfloat16 or wider, within the bound.
No kernel may reach another device: no remote copies, remote signals or barrier semaphores. Data moves between devices by JAX's collectives and lax.ppermute only.
A program may use at most 64 MiB of HBM per device.

```python
import jax
import jax.numpy as jnp
from jax import lax

B = 128
CW = 32
KP = 4
KA = 8
NB = 4
S = 4
LP = 64
OS = 16
CAP = 2
FB = 3072
N_GRP = 16
N_DOM = 48


def draw_a_cols(key, part):
    key = jax.random.fold_in(key, 11)
    devices = N_GRP * N_DOM
    key_left, key_right, key_kind, key_pick = jax.random.split(key, 4)
    left_count = jax.random.randint(key_left, (devices,), 1, S + 1).at[0].set(0)
    right_count = jax.random.randint(key_right, (devices,), 1, S + 1).at[devices - 1].set(0)
    row_device = jnp.arange(NB * devices) // NB
    row_within = jnp.arange(NB * devices) % NB
    lower = left_count[row_device][:, None]
    higher = right_count[row_device][:, None]
    kinds = jax.random.randint(key_kind, (NB * devices, KA), 0, 20)
    picks = jax.random.randint(key_pick, (NB * devices, KA), 0, 1 << 20)
    local = picks % NB
    from_lower = NB + picks % jnp.maximum(lower, 1)
    from_higher = NB + S + picks % jnp.maximum(higher, 1)
    padded = jnp.full_like(local, NB + 2 * S)
    chosen = jnp.where(kinds < 11, local, jnp.where(kinds < 14, jnp.where(lower > 0, from_lower, local), jnp.where(kinds < 17, jnp.where(higher > 0, from_higher, local), padded)))
    forced_lower = jnp.where(lower[:, 0] > 0, from_lower[:, 1], local[:, 1])
    forced_higher = jnp.where(higher[:, 0] > 0, from_higher[:, 1], local[:, 1])
    second = jnp.where(row_within == 0, forced_lower, jnp.where(row_within == NB - 1, forced_higher, chosen[:, 1]))
    chosen = chosen.at[:, 1].set(second)
    chosen = chosen.at[:, 0].set(local[:, 0])
    return chosen.astype(jnp.int32)


def draw_owner_slot(key, part):
    key = jax.random.fold_in(key, 23)
    devices = N_GRP * N_DOM
    key_first, key_order, key_slot = jax.random.split(key, 3)
    first = jax.random.randint(key_first, (devices, 1), 0, N_DOM)
    positions = jnp.arange(LP)
    offsets = positions // CAP
    owners = (first + offsets[None, :]) % N_DOM
    order_keys = jax.random.split(key_order, devices)
    orders = jax.vmap(lambda one_key: jax.random.permutation(one_key, LP))(order_keys)
    owners = jnp.take_along_axis(owners, orders, axis=1)
    groups = (jnp.arange(devices) // N_DOM)[:, None]
    within = jax.random.randint(key_slot, (devices, LP), 0, OS)
    return (owners * (N_GRP * OS) + groups * OS + within).reshape(devices * LP).astype(jnp.int32)


def set_ends(drawn, rng, low, top_value):
    longest = drawn.shape.index(max(drawn.shape))
    spots = []
    for shift in (0, 1):
        where = [jax.random.randint(jax.random.fold_in(rng, axis), (), 0, length) for axis, length in enumerate(drawn.shape)]
        where[longest] = (where[longest] + shift) % drawn.shape[longest]
        spots.append(tuple(where))
    return drawn.at[spots[0]].set(low).at[spots[1]].set(top_value)


def levels(key, shape, cuts, smallest, top_value):
    gain = 1.0
    for axis_at, blocks in cuts:
        heights = jax.random.uniform(jax.random.fold_in(jax.random.fold_in(key, 6), axis_at), (blocks,), jnp.float32, smallest / len(cuts), top_value / len(cuts))
        gain = gain * jnp.repeat(jnp.exp(heights), shape[axis_at] // blocks).reshape((-1,) + (1,) * (len(shape) - 1 - axis_at))
    return gain


def scatter_about(stream_key, extent, deviation, most, cuts=(), kind=jnp.bfloat16):
    gain = levels(stream_key, extent, cuts, -0.22, 0.18) if cuts else 1.0
    drawn = jax.random.normal(stream_key, extent, jnp.float32) * deviation * gain
    return jnp.minimum(jnp.maximum(drawn, -most), most).astype(kind)


def setup_inputs(seed: int = 0) -> dict:
    splits = jax.random.split(jax.random.key(seed), 7)
    return {
        "a_tiles": scatter_about(splits[0], (FB, KA, B, B), (KA * B) ** -0.5, 0.1875, ((0, 768),)),
        "a_cols": draw_a_cols(jax.random.fold_in(splits[6], 71), 0),
        "p_tiles": scatter_about(splits[2], (FB, B, KP * CW), 0.08, 0.47851562, ((0, 768),)),
        "send_list": set_ends(jax.random.randint(splits[3], (N_GRP * N_DOM, 2 * S), 0, NB), jax.random.fold_in(splits[3], 1), 0, NB - 1).astype(jnp.int32),
        "term_slot": set_ends(jax.random.randint(splits[4], (FB, KP, KA, KP), 0, LP), jax.random.fold_in(splits[4], 1), 0, LP - 1).astype(jnp.int32),
        "owner_slot": draw_owner_slot(jax.random.fold_in(splits[6], 71), 0),
    }


def reference(a_tiles, a_cols, p_tiles, send_list, term_slot, owner_slot):
    devices = N_GRP * N_DOM
    columns = KP * CW
    p_dev = p_tiles.reshape(devices, NB, B, columns)
    sends = jnp.take_along_axis(p_dev, send_list[:, :, None, None].astype(jnp.int32), axis=1)
    zero_side = jnp.zeros((1, S, B, columns), p_tiles.dtype)
    from_left = jnp.concatenate([zero_side, sends[:-1, S:]], 0)
    from_right = jnp.concatenate([sends[1:, :S], zero_side], 0)
    zero_block = jnp.zeros((devices, 1, B, columns), p_tiles.dtype)
    extended = jnp.concatenate([p_dev, from_left, from_right, zero_block], 1)
    a_dev = a_tiles.reshape(devices, NB, KA, B, B)
    cols_dev = a_cols.reshape(devices, NB, KA)
    slots_dev = term_slot.reshape(devices, NB * KP * KA * KP)

    def one_device(items):
        tiles, cols, table, own, slots = items
        gathered = table[cols].astype(jnp.float32)
        product = jnp.einsum('nark,nakc->nrac', tiles.astype(jnp.float32), gathered).astype(jnp.bfloat16)
        mine = own.reshape(NB, B, KP, CW).astype(jnp.float32)
        terms = jnp.einsum('nrqx,nrapy->nqapxy', mine, product.astype(jnp.float32).reshape(NB, B, KA, KP, CW))
        terms = terms.reshape(NB * KP * KA * KP, CW * CW)
        return jnp.zeros((LP, CW * CW), jnp.float32).at[slots].add(terms)

    partial_value = lax.map(one_device, (a_dev, cols_dev, extended, p_dev, slots_dev))
    coarse = jnp.zeros((N_DOM * N_GRP * OS, CW * CW), jnp.float32)
    return coarse.at[owner_slot].add(partial_value.reshape(devices * LP, CW * CW))
```

```python
import jax
import jax.numpy as jnp
from jax import lax
from jax.experimental import pallas as pl
from jax.experimental.pallas import tpu as pltpu
from jax.sharding import PartitionSpec as P

KA = 8
KP = 4
NB = 4
CW = 32
B = 128
LP = 64
OS = 16
CAP = 2
META = 128
SMALL = 4 * 1024 * 1024
MEDIUM = 16 * 1024 * 1024
PICK_GRANT = 60 * 1024 * 1024
VMEM = pltpu.VMEM
SMEM = pltpu.SMEM


def is_odd():
    return lax.rem(lax.axis_index("dom"), 2)


def pick_kernel(send_ref, p_ref, far_ref, near_ref):
    to_far = NB * is_odd()
    to_near = NB - to_far
    for k in range(NB):
        near_ref[k] = p_ref[send_ref[0, to_near + k]]
        far_ref[k] = p_ref[send_ref[0, to_far + k]]


def pick(send_list, p_tiles):
    shape = jax.ShapeDtypeStruct(p_tiles.shape, p_tiles.dtype)
    return pl.pallas_call(
        pick_kernel,
        out_shape=(shape, shape),
        in_specs=[pl.BlockSpec(memory_space=SMEM), pl.BlockSpec(memory_space=VMEM)],
        out_specs=(pl.BlockSpec(memory_space=VMEM),) * 2,
        compiler_params=pltpu.CompilerParams(vmem_limit_bytes=PICK_GRANT),
    )(send_list, p_tiles)


def lane_turn(v):
    lane = lax.broadcasted_iota(jnp.int32, (8, B), 1)
    low = lane < 64
    even = (lane % 64) < 32

    def swap(a, b, mask, shift):
        moved = pltpu.roll(jnp.where(mask, b, a), shift, 1)
        return jnp.where(mask, a, moved), jnp.where(mask, moved, b)

    def swap_near(a, b):
        first = jnp.where(even, a, pltpu.roll(b, 32, 1))
        second = jnp.where(even, pltpu.roll(a, 96, 1), b)
        return first, second

    v0, v2 = swap(v[0], v[2], low, 64)
    v1, v3 = swap(v[1], v[3], low, 64)
    v0, v1 = swap_near(v0, v1)
    v2, v3 = swap_near(v2, v3)
    return v0, v1, v2, v3


def add_terms(accs, places, terms):
    rows = [pl.ds(pl.multiple_of(place * 8, 8), 8) for place in places]
    sums = [acc[at, :] + term for acc, at, term in zip(accs, rows, terms)]
    for acc, at, value in zip(accs, rows, sums):
        acc[at, :] = value


def terms_kernel(cols_ref, slots_ref, pos_ref, meta_ref, a_ref, p_ref, far_ref, near_ref, out_ref, table, product, *accs):
    table[0:4] = p_ref[...]
    odd = is_odd()
    table[pl.ds(2 * NB - NB * odd, NB)] = near_ref[...]
    table[pl.ds(NB + NB * odd, NB)] = far_ref[...]
    table[3 * NB] = jnp.zeros((B, B), jnp.bfloat16)
    for acc in accs:
        acc[...] = jnp.zeros_like(acc)
    row = lax.broadcasted_iota(jnp.int32, (B, B), 0)
    column = lax.broadcasted_iota(jnp.int32, (B, B), 1)
    source = (row // 32) * 32 + 4 * (row % 8) + (row % 32) // 8
    turn = (column == source).astype(jnp.bfloat16)
    for n in range(NB):
        turned = lax.dot_general(turn, p_ref[n], (((1,), (1,)), ((), ())), preferred_element_type=jnp.float32).astype(jnp.bfloat16)
        for a in range(KA):
            product[n, :, a * B : (a + 1) * B] = jnp.dot(
                a_ref[n, a], table[cols_ref[n, a]], preferred_element_type=jnp.float32
            ).astype(jnp.bfloat16)
        for a in range(0, KA, 2):
            tiles = jnp.dot(turned, product[n, :, a * B : (a + 2) * B], preferred_element_type=jnp.float32)
            for half in range(2):
                tile = tiles[:, half * B : (half + 1) * B]
                for q in range(KP):
                    v = [tile[q * 32 + 8 * j : q * 32 + 8 * j + 8] for j in range(4)]
                    first = ((n * KP + q) * KA + a + half) * KP
                    add_terms(accs, [pos_ref[slots_ref[first + p]] for p in range(KP)], lane_turn(v))
    count = out_ref.shape[0]
    for i in range(8):
        parts = [acc[pl.ds(i, count, stride=8), :] for acc in accs]
        total = (parts[0] + parts[1]) + (parts[2] + parts[3])
        out_ref[:, i * B : (i + 1) * B] = total.astype(jnp.bfloat16)
    out_ref[:, 8 * B :] = meta_ref[...]


def send_blocks(a_cols, slots, pos, meta, a_tiles, p_tiles, far, near):
    count = meta.shape[0]
    vmem = pl.BlockSpec(memory_space=VMEM)
    smem = pl.BlockSpec(memory_space=SMEM)
    return pl.pallas_call(
        terms_kernel,
        out_shape=jax.ShapeDtypeStruct((count, 8 * B + META), jnp.bfloat16),
        in_specs=[smem, smem, smem, vmem, vmem, vmem, vmem, vmem],
        out_specs=vmem,
        scratch_shapes=[
            VMEM((3 * NB + 1, B, B), jnp.bfloat16),
            VMEM((NB, B, KA * B), jnp.bfloat16),
        ]
        + [VMEM((count * 8, B), jnp.float32)] * KP,
        compiler_params=pltpu.CompilerParams(vmem_limit_bytes=MEDIUM),
        cost_estimate=pl.CostEstimate(flops=300_000_000, bytes_accessed=2_000_000, transcendentals=0),
    )(a_cols, slots, pos, meta, a_tiles, p_tiles, far, near)


def owner_kernel(in_ref, out_ref):
    within = in_ref[:, 8 * B :].astype(jnp.float32)
    lane = lax.broadcasted_iota(jnp.int32, within.shape, 1).astype(jnp.float32)
    place = jnp.where(within == lane, 1.0, 0.0).T[:OS].astype(jnp.bfloat16)
    out_ref[...] = jnp.dot(place, in_ref[:, : 8 * B], preferred_element_type=jnp.float32).astype(jnp.bfloat16)


def own_sum(received):
    return pl.pallas_call(
        owner_kernel,
        out_shape=jax.ShapeDtypeStruct((OS, 8 * B), jnp.bfloat16),
        in_specs=[pl.BlockSpec(memory_space=VMEM)],
        out_specs=pl.BlockSpec(memory_space=VMEM),
        compiler_params=pltpu.CompilerParams(vmem_limit_bytes=SMALL),
    )(received)


def body(a_tiles, a_cols, p_tiles, send_list, term_slot, owner_slot):
    dom_count = lax.axis_size("dom")
    grp_count = lax.axis_size("grp")
    devices = dom_count * grp_count
    to_far, to_near = pick(send_list, p_tiles)
    near = [(i, i ^ 1) for i in range(devices)]
    far = [(i, ((i + 1) ^ 1) - 1) for i in range(1, devices - 1)]
    from_far = lax.ppermute(to_far, ("grp", "dom"), far)
    from_near = lax.ppermute(to_near, ("grp", "dom"), near)

    rows = dom_count * CAP
    owner = owner_slot // (grp_count * OS)
    within = owner_slot % OS
    index = jnp.arange(LP)
    same = (owner[:, None] == owner[None, :]) & (index[None, :] < index[:, None])
    pos = owner * CAP + jnp.sum(same.astype(jnp.int32), axis=1)
    here = pos[None, :] == jnp.arange(rows)[:, None]
    meta = jnp.sum(jnp.where(here, within[None, :], 0), axis=1).astype(jnp.bfloat16)
    meta = jnp.broadcast_to(meta[:, None], (rows, META))

    blocks = send_blocks(a_cols, term_slot.reshape(-1), pos, meta, a_tiles, p_tiles, from_far, from_near)
    received = lax.all_to_all(blocks, "dom", 0, 0, tiled=True)
    owned = own_sum(received)
    return lax.all_gather(owned, "grp", axis=0, tiled=True).astype(jnp.float32)


def solution(mesh):
    placed = (
        P(("grp", "dom"), None, None, None),
        P(("grp", "dom"), None),
        P(("grp", "dom"), None, None),
        P(("grp", "dom"), None),
        P(("grp", "dom"), None, None, None),
        P(("grp", "dom")),
    )
    return jax.shard_map(
        body, mesh=mesh, in_specs=placed, out_specs=P("dom", None), check_vma=False
    )
```

```python
import jax
import jax.numpy as jnp
from jax import lax
from jax.experimental import pallas as pl
from jax.experimental.pallas import tpu as pltpu
from jax.sharding import PartitionSpec as P

KA = 8
KP = 4
NB = 4
CW = 32
B = 128
LP = 64
OS = 16
CAP = 2
META = 128
SMALL = 4 * 1024 * 1024
MEDIUM = 16 * 1024 * 1024
PICK_GRANT = 60 * 1024 * 1024
VMEM = pltpu.VMEM
SMEM = pltpu.SMEM


def is_odd():
    return lax.rem(lax.axis_index("dom"), 2)


def pick_kernel(send_ref, p_ref, far_ref, near_ref):
    to_far = NB * is_odd()
    to_near = NB - to_far
    for k in range(NB):
        near_ref[k] = p_ref[send_ref[0, to_near + k]]
        far_ref[k] = p_ref[send_ref[0, to_far + k]]


def pick(send_list, p_tiles):
    shape = jax.ShapeDtypeStruct(p_tiles.shape, p_tiles.dtype)
    return pl.pallas_call(
        pick_kernel,
        out_shape=(shape, shape),
        in_specs=[pl.BlockSpec(memory_space=SMEM), pl.BlockSpec(memory_space=VMEM)],
        out_specs=(pl.BlockSpec(memory_space=VMEM),) * 2,
        compiler_params=pltpu.CompilerParams(vmem_limit_bytes=PICK_GRANT),
    )(send_list, p_tiles)


def lane_turn(v):
    lane = lax.broadcasted_iota(jnp.int32, (8, B), 1)
    low = lane < 64
    even = (lane % 64) < 32

    def swap(a, b, mask, shift):
        moved = pltpu.roll(jnp.where(mask, b, a), shift, 1)
        return jnp.where(mask, a, moved), jnp.where(mask, moved, b)

    def swap_near(a, b):
        first = jnp.where(even, a, pltpu.roll(b, 32, 1))
        second = jnp.where(even, pltpu.roll(a, 96, 1), b)
        return first, second

    v0, v2 = swap(v[0], v[2], low, 64)
    v1, v3 = swap(v[1], v[3], low, 64)
    v0, v1 = swap_near(v0, v1)
    v2, v3 = swap_near(v2, v3)
    return v0, v1, v2, v3


def turn_kernel(a_ref, p_ref, turned_ref):
    row = lax.broadcasted_iota(jnp.int32, (B, B), 0)
    column = lax.broadcasted_iota(jnp.int32, (B, B), 1)
    source = (row // 32) * 32 + 4 * (row % 8) + (row % 32) // 8
    turn = (column == source).astype(jnp.bfloat16)
    for n in range(NB):
        turned_ref[n] = lax.dot_general(turn, p_ref[n], (((1,), (1,)), ((), ())), preferred_element_type=jnp.float32).astype(jnp.bfloat16)


def turn_blocks(a_tiles, p_tiles):
    vmem = pl.BlockSpec(memory_space=VMEM)
    return pl.pallas_call(
        turn_kernel,
        out_shape=jax.ShapeDtypeStruct(p_tiles.shape, p_tiles.dtype),
        in_specs=[vmem, vmem],
        out_specs=vmem,
        compiler_params=pltpu.CompilerParams(vmem_limit_bytes=MEDIUM),
        cost_estimate=pl.CostEstimate(flops=20_000_000, bytes_accessed=1_400_000, transcendentals=0),
    )(a_tiles, p_tiles)


def add_terms(accs, places, terms):
    rows = [pl.ds(pl.multiple_of(place * 8, 8), 8) for place in places]
    sums = [acc[at, :] + term for acc, at, term in zip(accs, rows, terms)]
    for acc, at, value in zip(accs, rows, sums):
        acc[at, :] = value


def terms_kernel(cols_ref, slots_ref, pos_ref, meta_ref, a_ref, p_ref, turned_ref, far_ref, near_ref, out_ref, table, product, *accs):
    table[0:4] = p_ref[...]
    odd = is_odd()
    table[pl.ds(2 * NB - NB * odd, NB)] = near_ref[...]
    table[pl.ds(NB + NB * odd, NB)] = far_ref[...]
    table[3 * NB] = jnp.zeros((B, B), jnp.bfloat16)
    for acc in accs:
        acc[...] = jnp.zeros_like(acc)
    for n in range(NB):
        turned = turned_ref[n]
        for a in range(KA):
            product[n, :, a * B : (a + 1) * B] = jnp.dot(
                a_ref[n, a], table[cols_ref[n, a]], preferred_element_type=jnp.float32
            ).astype(jnp.bfloat16)
        for a in range(0, KA, 2):
            tiles = jnp.dot(turned, product[n, :, a * B : (a + 2) * B], preferred_element_type=jnp.float32)
            for half in range(2):
                tile = tiles[:, half * B : (half + 1) * B]
                for q in range(KP):
                    v = [tile[q * 32 + 8 * j : q * 32 + 8 * j + 8] for j in range(4)]
                    first = ((n * KP + q) * KA + a + half) * KP
                    add_terms(accs, [pos_ref[slots_ref[first + p]] for p in range(KP)], lane_turn(v))
    count = out_ref.shape[0]
    for i in range(8):
        parts = [acc[pl.ds(i, count, stride=8), :] for acc in accs]
        total = (parts[0] + parts[1]) + (parts[2] + parts[3])
        out_ref[:, i * B : (i + 1) * B] = total.astype(jnp.bfloat16)
    out_ref[:, 8 * B :] = meta_ref[...]


def send_blocks(a_cols, slots, pos, meta, a_tiles, p_tiles, turned, far, near):
    count = meta.shape[0]
    vmem = pl.BlockSpec(memory_space=VMEM)
    smem = pl.BlockSpec(memory_space=SMEM)
    return pl.pallas_call(
        terms_kernel,
        out_shape=jax.ShapeDtypeStruct((count, 8 * B + META), jnp.bfloat16),
        in_specs=[smem, smem, smem, vmem, vmem, vmem, vmem, vmem, vmem],
        out_specs=vmem,
        scratch_shapes=[
            VMEM((3 * NB + 1, B, B), jnp.bfloat16),
            VMEM((NB, B, KA * B), jnp.bfloat16),
        ]
        + [VMEM((count * 8, B), jnp.float32)] * KP,
        compiler_params=pltpu.CompilerParams(vmem_limit_bytes=MEDIUM),
        cost_estimate=pl.CostEstimate(flops=300_000_000, bytes_accessed=2_000_000, transcendentals=0),
    )(a_cols, slots, pos, meta, a_tiles, p_tiles, turned, far, near)


def owner_kernel(in_ref, out_ref):
    within = in_ref[:, 8 * B :].astype(jnp.float32)
    lane = lax.broadcasted_iota(jnp.int32, within.shape, 1).astype(jnp.float32)
    place = jnp.where(within == lane, 1.0, 0.0).T[:OS].astype(jnp.bfloat16)
    out_ref[...] = jnp.dot(place, in_ref[:, : 8 * B], preferred_element_type=jnp.float32).astype(jnp.bfloat16)


def own_sum(received):
    return pl.pallas_call(
        owner_kernel,
        out_shape=jax.ShapeDtypeStruct((OS, 8 * B), jnp.bfloat16),
        in_specs=[pl.BlockSpec(memory_space=VMEM)],
        out_specs=pl.BlockSpec(memory_space=VMEM),
        compiler_params=pltpu.CompilerParams(vmem_limit_bytes=SMALL),
    )(received)


def body(a_tiles, a_cols, p_tiles, send_list, term_slot, owner_slot):
    dom_count = lax.axis_size("dom")
    grp_count = lax.axis_size("grp")
    devices = dom_count * grp_count
    to_far, to_near = pick(send_list, p_tiles)
    near = [(i, i ^ 1) for i in range(devices)]
    far = [(i, ((i + 1) ^ 1) - 1) for i in range(1, devices - 1)]
    from_far = lax.ppermute(to_far, ("grp", "dom"), far)
    from_near = lax.ppermute(to_near, ("grp", "dom"), near)

    turned = turn_blocks(a_tiles, p_tiles)
    rows = dom_count * CAP
    owner = owner_slot // (grp_count * OS)
    within = owner_slot % OS
    index = jnp.arange(LP)
    same = (owner[:, None] == owner[None, :]) & (index[None, :] < index[:, None])
    pos = owner * CAP + jnp.sum(same.astype(jnp.int32), axis=1)
    here = pos[None, :] == jnp.arange(rows)[:, None]
    meta = jnp.sum(jnp.where(here, within[None, :], 0), axis=1).astype(jnp.bfloat16)
    meta = jnp.broadcast_to(meta[:, None], (rows, META))

    blocks = send_blocks(a_cols, term_slot.reshape(-1), pos, meta, a_tiles, p_tiles, turned, from_far, from_near)
    received = lax.all_to_all(blocks, "dom", 0, 0, tiled=True)
    owned = own_sum(received)
    return lax.all_gather(owned, "grp", axis=0, tiled=True).astype(jnp.float32)


def solution(mesh):
    placed = (
        P(("grp", "dom"), None, None, None),
        P(("grp", "dom"), None),
        P(("grp", "dom"), None, None),
        P(("grp", "dom"), None),
        P(("grp", "dom"), None, None, None),
        P(("grp", "dom")),
    )
    return jax.shard_map(
        body, mesh=mesh, in_specs=placed, out_specs=P("dom", None), check_vma=False
    )
```

```python
import jax
import jax.numpy as jnp
from jax import lax
from jax.experimental import pallas as pl
from jax.experimental.pallas import tpu as pltpu
from jax.sharding import PartitionSpec as P

KA = 8
KP = 4
NB = 4
CW = 32
B = 128
LP = 64
OS = 16
CAP = 2
META = 128
SMALL = 4 * 1024 * 1024
MEDIUM = 16 * 1024 * 1024
VMEM = pltpu.VMEM
SMEM = pltpu.SMEM


def is_odd():
    return lax.rem(lax.axis_index("dom"), 2)


def chosen(entries, p_tiles):
    picked = jnp.broadcast_to(p_tiles[NB - 1], p_tiles.shape)
    for k in range(NB - 1):
        picked = jnp.where(entries[:, None, None] == k, p_tiles[k], picked)
    return picked


def lane_turn(v):
    lane = lax.broadcasted_iota(jnp.int32, (8, B), 1)
    low = lane < 64
    even = (lane % 64) < 32

    def swap(a, b, mask, shift):
        moved = pltpu.roll(jnp.where(mask, b, a), shift, 1)
        return jnp.where(mask, a, moved), jnp.where(mask, moved, b)

    def swap_near(a, b):
        first = jnp.where(even, a, pltpu.roll(b, 32, 1))
        second = jnp.where(even, pltpu.roll(a, 96, 1), b)
        return first, second

    v0, v2 = swap(v[0], v[2], low, 64)
    v1, v3 = swap(v[1], v[3], low, 64)
    v0, v1 = swap_near(v0, v1)
    v2, v3 = swap_near(v2, v3)
    return v0, v1, v2, v3


def turn_kernel(a_ref, p_ref, turned_ref):
    row = lax.broadcasted_iota(jnp.int32, (B, B), 0)
    column = lax.broadcasted_iota(jnp.int32, (B, B), 1)
    source = (row // 32) * 32 + 4 * (row % 8) + (row % 32) // 8
    turn = (column == source).astype(jnp.bfloat16)
    for n in range(NB):
        turned_ref[n] = lax.dot_general(turn, p_ref[n], (((1,), (1,)), ((), ())), preferred_element_type=jnp.float32).astype(jnp.bfloat16)


def turn_blocks(a_tiles, p_tiles):
    vmem = pl.BlockSpec(memory_space=VMEM)
    return pl.pallas_call(
        turn_kernel,
        out_shape=jax.ShapeDtypeStruct(p_tiles.shape, p_tiles.dtype),
        in_specs=[vmem, vmem],
        out_specs=vmem,
        compiler_params=pltpu.CompilerParams(vmem_limit_bytes=MEDIUM),
        cost_estimate=pl.CostEstimate(flops=20_000_000, bytes_accessed=1_400_000, transcendentals=0),
    )(a_tiles, p_tiles)


def add_terms(accs, places, terms):
    rows = [pl.ds(pl.multiple_of(place * 8, 8), 8) for place in places]
    sums = [acc[at, :] + term for acc, at, term in zip(accs, rows, terms)]
    for acc, at, value in zip(accs, rows, sums):
        acc[at, :] = value


def terms_kernel(cols_ref, slots_ref, pos_ref, meta_ref, a_ref, p_ref, turned_ref, near_ref, far_ref, out_ref, table, product, *accs):
    table[0:4] = p_ref[...]
    odd = is_odd()
    table[pl.ds(2 * NB - NB * odd, NB)] = near_ref[...]
    table[pl.ds(NB + NB * odd, NB)] = far_ref[...]
    table[3 * NB] = jnp.zeros((B, B), jnp.bfloat16)
    for acc in accs:
        acc[...] = jnp.zeros_like(acc)
    for n in range(NB):
        turned = turned_ref[n]
        for a in range(KA):
            product[n, :, a * B : (a + 1) * B] = jnp.dot(
                a_ref[n, a], table[cols_ref[n, a]], preferred_element_type=jnp.float32
            ).astype(jnp.bfloat16)
        for a in range(0, KA, 2):
            tiles = jnp.dot(turned, product[n, :, a * B : (a + 2) * B], preferred_element_type=jnp.float32)
            for half in range(2):
                tile = tiles[:, half * B : (half + 1) * B]
                for q in range(KP):
                    v = [tile[q * 32 + 8 * j : q * 32 + 8 * j + 8] for j in range(4)]
                    first = ((n * KP + q) * KA + a + half) * KP
                    add_terms(accs, [pos_ref[slots_ref[first + p]] for p in range(KP)], lane_turn(v))
    count = out_ref.shape[0]
    first = accs[0]
    first[...] = (accs[0][...] + accs[1][...]) + (accs[2][...] + accs[3][...])
    for i in range(8):
        out_ref[:, i * B : (i + 1) * B] = first[pl.ds(i, count, stride=8), :].astype(jnp.bfloat16)
    out_ref[:, 8 * B :] = meta_ref[...]


def send_blocks(a_cols, slots, pos, meta, a_tiles, p_tiles, turned, near, far):
    count = meta.shape[0]
    vmem = pl.BlockSpec(memory_space=VMEM)
    smem = pl.BlockSpec(memory_space=SMEM)
    return pl.pallas_call(
        terms_kernel,
        out_shape=jax.ShapeDtypeStruct((count, 8 * B + META), jnp.bfloat16),
        in_specs=[smem, smem, smem, vmem, vmem, vmem, vmem, vmem, vmem],
        out_specs=vmem,
        scratch_shapes=[
            VMEM((3 * NB + 1, B, B), jnp.bfloat16),
            VMEM((NB, B, KA * B), jnp.bfloat16),
        ]
        + [VMEM((count * 8, B), jnp.float32)] * KP,
        compiler_params=pltpu.CompilerParams(vmem_limit_bytes=MEDIUM),
        cost_estimate=pl.CostEstimate(flops=300_000_000, bytes_accessed=2_000_000, transcendentals=0),
    )(a_cols, slots, pos, meta, a_tiles, p_tiles, turned, near, far)


def owner_kernel(in_ref, out_ref):
    within = in_ref[:, 8 * B :].astype(jnp.float32)
    lane = lax.broadcasted_iota(jnp.int32, within.shape, 1).astype(jnp.float32)
    place = jnp.where(within == lane, 1.0, 0.0).T[:OS].astype(jnp.bfloat16)
    out_ref[...] = jnp.dot(place, in_ref[:, : 8 * B], preferred_element_type=jnp.float32).astype(jnp.bfloat16)


def own_sum(received):
    return pl.pallas_call(
        owner_kernel,
        out_shape=jax.ShapeDtypeStruct((OS, 8 * B), jnp.bfloat16),
        in_specs=[pl.BlockSpec(memory_space=VMEM)],
        out_specs=pl.BlockSpec(memory_space=VMEM),
        compiler_params=pltpu.CompilerParams(vmem_limit_bytes=SMALL),
    )(received)


def body(a_tiles, a_cols, p_tiles, send_list, term_slot, owner_slot):
    dom_count = lax.axis_size("dom")
    grp_count = lax.axis_size("grp")
    devices = dom_count * grp_count
    odd = is_odd() == 1
    to_lower, to_higher = send_list[0, :NB], send_list[0, NB:]
    to_far = chosen(jnp.where(odd, to_higher, to_lower), p_tiles)
    to_near = chosen(jnp.where(odd, to_lower, to_higher), p_tiles)
    near = [(i, i ^ 1) for i in range(devices)]
    far = [(i, ((i + 1) ^ 1) - 1) for i in range(1, devices - 1)]
    from_far = lax.ppermute(to_far, ("grp", "dom"), far)
    from_near = lax.ppermute(to_near, ("grp", "dom"), near)

    turned = turn_blocks(a_tiles, p_tiles)
    rows = dom_count * CAP
    owner = owner_slot // (grp_count * OS)
    within = owner_slot % OS
    index = jnp.arange(LP)
    same = (owner[:, None] == owner[None, :]) & (index[None, :] < index[:, None])
    pos = owner * CAP + jnp.sum(same.astype(jnp.int32), axis=1)
    here = pos[None, :] == jnp.arange(rows)[:, None]
    meta = jnp.sum(jnp.where(here, within[None, :], 0), axis=1).astype(jnp.bfloat16)
    meta = jnp.broadcast_to(meta[:, None], (rows, META))

    blocks = send_blocks(a_cols, term_slot.reshape(-1), pos, meta, a_tiles, p_tiles, turned, from_near, from_far)
    received = lax.all_to_all(blocks, "dom", 0, 0, tiled=True)
    owned = own_sum(received)
    return lax.all_gather(owned, "grp", axis=0, tiled=True).astype(jnp.float32)


def solution(mesh):
    placed = (
        P(("grp", "dom"), None, None, None),
        P(("grp", "dom"), None),
        P(("grp", "dom"), None, None),
        P(("grp", "dom"), None),
        P(("grp", "dom"), None, None, None),
        P(("grp", "dom")),
    )
    return jax.shard_map(
        body, mesh=mesh, in_specs=placed, out_specs=P("dom", None), check_vma=False
    )
```

```python
import jax
import jax.numpy as jnp
from jax import lax
from jax.experimental import pallas as pl
from jax.experimental.pallas import tpu as pltpu
from jax.sharding import PartitionSpec as P

KA = 8
KP = 4
NB = 4
CW = 32
B = 128
LP = 64
OS = 16
CAP = 2
META = 128
PARTS = 4
SMALL = 4 * 1024 * 1024
MEDIUM = 16 * 1024 * 1024
VMEM = pltpu.VMEM
SMEM = pltpu.SMEM


def is_odd():
    return lax.rem(lax.axis_index("dom"), 2)


def chosen(entries, p_tiles):
    picked = jnp.broadcast_to(p_tiles[NB - 1], p_tiles.shape)
    for k in range(NB - 1):
        picked = jnp.where(entries[:, None, None] == k, p_tiles[k], picked)
    return picked


def lane_turn(v):
    lane = lax.broadcasted_iota(jnp.int32, (8, B), 1)
    low = lane < 64
    even = (lane % 64) < 32

    def swap(a, b, mask, shift):
        moved = pltpu.roll(jnp.where(mask, b, a), shift, 1)
        return jnp.where(mask, a, moved), jnp.where(mask, moved, b)

    def swap_near(a, b):
        first = jnp.where(even, a, pltpu.roll(b, 32, 1))
        second = jnp.where(even, pltpu.roll(a, 96, 1), b)
        return first, second

    v0, v2 = swap(v[0], v[2], low, 64)
    v1, v3 = swap(v[1], v[3], low, 64)
    v0, v1 = swap_near(v0, v1)
    v2, v3 = swap_near(v2, v3)
    return v0, v1, v2, v3


def turn_kernel(a_ref, p_ref, turned_ref):
    row = lax.broadcasted_iota(jnp.int32, (B, B), 0)
    column = lax.broadcasted_iota(jnp.int32, (B, B), 1)
    source = (row // 32) * 32 + 4 * (row % 8) + (row % 32) // 8
    turn = (column == source).astype(jnp.bfloat16)
    for n in range(NB):
        turned_ref[n] = lax.dot_general(turn, p_ref[n], (((1,), (1,)), ((), ())), preferred_element_type=jnp.float32).astype(jnp.bfloat16)


def turn_blocks(a_tiles, p_tiles):
    vmem = pl.BlockSpec(memory_space=VMEM)
    return pl.pallas_call(
        turn_kernel,
        out_shape=jax.ShapeDtypeStruct(p_tiles.shape, p_tiles.dtype),
        in_specs=[vmem, vmem],
        out_specs=vmem,
        compiler_params=pltpu.CompilerParams(vmem_limit_bytes=MEDIUM),
        cost_estimate=pl.CostEstimate(flops=20_000_000, bytes_accessed=1_400_000, transcendentals=0),
    )(a_tiles, p_tiles)


def add_terms(accs, places, terms):
    rows = [pl.ds(pl.multiple_of(place * 8, 8), 8) for place in places]
    sums = [acc[at, :] + term for acc, at, term in zip(accs, rows, terms)]
    for acc, at, value in zip(accs, rows, sums):
        acc[at, :] = value


def terms_kernel(cols_ref, slots_ref, pos_ref, meta_ref, a_ref, p_ref, turned_ref, near_ref, far_ref, out_ref, table, product, *accs):
    table[0:4] = p_ref[...]
    odd = is_odd()
    table[pl.ds(2 * NB - NB * odd, NB)] = near_ref[...]
    table[pl.ds(NB + NB * odd, NB)] = far_ref[...]
    table[3 * NB] = jnp.zeros((B, B), jnp.bfloat16)
    for acc in accs:
        acc[...] = jnp.zeros_like(acc)
    for n in range(NB):
        turned = turned_ref[n]
        for a in range(KA):
            product[n, :, a * B : (a + 1) * B] = jnp.dot(
                a_ref[n, a], table[cols_ref[n, a]], preferred_element_type=jnp.float32
            ).astype(jnp.bfloat16)
        for a in range(0, KA, 2):
            tiles = jnp.dot(turned, product[n, :, a * B : (a + 2) * B], preferred_element_type=jnp.float32)
            for half in range(2):
                tile = tiles[:, half * B : (half + 1) * B]
                for q in range(KP):
                    v = [tile[q * 32 + 8 * j : q * 32 + 8 * j + 8] for j in range(4)]
                    first = ((n * KP + q) * KA + a + half) * KP
                    add_terms(accs, [pos_ref[slots_ref[first + p]] for p in range(KP)], lane_turn(v))
    count = out_ref.shape[0]
    first = accs[0]
    first[...] = (accs[0][...] + accs[1][...]) + (accs[2][...] + accs[3][...])
    for i in range(8):
        out_ref[:, i * B : (i + 1) * B] = first[pl.ds(i, count, stride=8), :].astype(jnp.bfloat16)
    out_ref[:, 8 * B :] = meta_ref[...]


def send_blocks(a_cols, slots, pos, meta, a_tiles, p_tiles, turned, near, far):
    count = meta.shape[0]
    vmem = pl.BlockSpec(memory_space=VMEM)
    smem = pl.BlockSpec(memory_space=SMEM)
    return pl.pallas_call(
        terms_kernel,
        out_shape=jax.ShapeDtypeStruct((count, 8 * B + META), jnp.bfloat16),
        in_specs=[smem, smem, smem, vmem, vmem, vmem, vmem, vmem, vmem],
        out_specs=vmem,
        scratch_shapes=[
            VMEM((3 * NB + 1, B, B), jnp.bfloat16),
            VMEM((NB, B, KA * B), jnp.bfloat16),
        ]
        + [VMEM((count * 8, B), jnp.float32)] * KP,
        compiler_params=pltpu.CompilerParams(vmem_limit_bytes=MEDIUM),
        cost_estimate=pl.CostEstimate(flops=300_000_000, bytes_accessed=2_000_000, transcendentals=0),
    )(a_cols, slots, pos, meta, a_tiles, p_tiles, turned, near, far)


def owner_kernel(in_ref, out_ref):
    within = in_ref[:, 8 * B :].astype(jnp.float32)
    lane = lax.broadcasted_iota(jnp.int32, within.shape, 1).astype(jnp.float32)
    place = jnp.where(within == lane, 1.0, 0.0).T[:OS].astype(jnp.bfloat16)
    out_ref[...] = jnp.dot(place, in_ref[:, : 8 * B], preferred_element_type=jnp.float32).astype(jnp.bfloat16)


def own_sum(received):
    return pl.pallas_call(
        owner_kernel,
        out_shape=jax.ShapeDtypeStruct((OS, 8 * B), jnp.bfloat16),
        in_specs=[pl.BlockSpec(memory_space=VMEM)],
        out_specs=pl.BlockSpec(memory_space=VMEM),
        compiler_params=pltpu.CompilerParams(vmem_limit_bytes=SMALL),
    )(received)


def widen_kernel(in_ref, out_ref, wide, sems):
    rows = in_ref.shape[0] // PARTS
    copies = []
    for i in range(PARTS):
        at = pl.ds(i * rows, rows)
        wide[at, :] = in_ref[at, :].astype(jnp.float32)
        copies.append(pltpu.make_async_copy(wide.at[at], out_ref.at[at], sems.at[i]))
        copies[-1].start()
    for copy in copies:
        copy.wait()


def widen(gathered):
    return pl.pallas_call(
        widen_kernel,
        out_shape=jax.ShapeDtypeStruct(gathered.shape, jnp.float32),
        in_specs=[pl.BlockSpec(memory_space=VMEM)],
        out_specs=pl.BlockSpec(memory_space=pltpu.HBM),
        scratch_shapes=[VMEM(gathered.shape, jnp.float32), pltpu.SemaphoreType.DMA((PARTS,))],
        compiler_params=pltpu.CompilerParams(vmem_limit_bytes=MEDIUM),
    )(gathered)


def body(a_tiles, a_cols, p_tiles, send_list, term_slot, owner_slot):
    dom_count = lax.axis_size("dom")
    grp_count = lax.axis_size("grp")
    devices = dom_count * grp_count
    odd = is_odd() == 1
    to_lower, to_higher = send_list[0, :NB], send_list[0, NB:]
    to_far = chosen(jnp.where(odd, to_higher, to_lower), p_tiles)
    to_near = chosen(jnp.where(odd, to_lower, to_higher), p_tiles)
    near = [(i, i ^ 1) for i in range(devices)]
    far = [(i, ((i + 1) ^ 1) - 1) for i in range(1, devices - 1)]
    from_far = lax.ppermute(to_far, ("grp", "dom"), far)
    from_near = lax.ppermute(to_near, ("grp", "dom"), near)

    turned = turn_blocks(a_tiles, p_tiles)
    rows = dom_count * CAP
    owner = owner_slot // (grp_count * OS)
    within = owner_slot % OS
    index = jnp.arange(LP)
    same = (owner[:, None] == owner[None, :]) & (index[None, :] < index[:, None])
    pos = owner * CAP + jnp.sum(same.astype(jnp.int32), axis=1)
    here = pos[None, :] == jnp.arange(rows)[:, None]
    meta = jnp.sum(jnp.where(here, within[None, :], 0), axis=1).astype(jnp.bfloat16)
    meta = jnp.broadcast_to(meta[:, None], (rows, META))

    blocks = send_blocks(a_cols, term_slot.reshape(-1), pos, meta, a_tiles, p_tiles, turned, from_near, from_far)
    received = lax.all_to_all(blocks, "dom", 0, 0, tiled=True)
    owned = own_sum(received)
    return widen(lax.all_gather(owned, "grp", axis=0, tiled=True))


def solution(mesh):
    placed = (
        P(("grp", "dom"), None, None, None),
        P(("grp", "dom"), None),
        P(("grp", "dom"), None, None),
        P(("grp", "dom"), None),
        P(("grp", "dom"), None, None, None),
        P(("grp", "dom")),
    )
    return jax.shard_map(
        body, mesh=mesh, in_specs=placed, out_specs=P("dom", None), check_vma=False
    )
```
